32 devices in a mesh: groups: 2 (over y), aux: 4 (over z), pts: 2 (over x), rep: 2 (over core).
Axes of the slice: x: 2, y: 2, z: 4, core: 2. Of those that a mesh axis runs over, the one named last changes fastest.
Arguments:
- density_slab: bfloat16 [32, 1024, 1024], P('groups', 'aux', 'rep'), parts along dimension 0, may hold values from -0.005859375 to 0.005859375
- orbitals: bfloat16 [2048, 8192], P(('groups', 'rep'), 'pts'), parts along dimension 0, may hold values from -6 to 6
Outputs:
- rhs_share: float32 [16384, 8192], P(('groups', 'pts'), ('aux', 'rep')), parts along dimension 0
The draws below stay inside these ranges and needn't reach their ends.
There are 2 independent parts, one for each index of `groups`. The reference program is written for one: setup_inputs(seed, part) draws one part's arguments, and reference() takes and returns one part's arrays. A program takes and returns all parts, laid end to end along the dimension named above; each array names one. Nothing has to cross between parts.
All inputs are finite; a program needn't handle non-finite values.
Results may differ from the reference program's by a relative error of at most 0.0003.
Values may be sent and summed in bfloat16 or wider, within the bound.
No kernel may reach another device: no remote copies, remote signals or barrier semaphores. Data moves between devices by JAX's collectives and lax.ppermute only.
A program may use at most 64 MiB of HBM per device.

```python
import jax
import jax.numpy as jnp
from jax import lax

NBF = 1024
NPTS = 8192
AUX = 16


def block_levels(own_key, extent, shards, smallest, largest):
    level = 1.0
    for dim, parts in shards:
        heights = jax.random.uniform(jax.random.fold_in(jax.random.fold_in(own_key, 6), dim), (parts,), jnp.float32, smallest / len(shards), largest / len(shards))
        level = level * jnp.repeat(jnp.exp(heights), extent[dim] // parts).reshape((-1,) + (1,) * (len(extent) - 1 - dim))
    return level


def noise(own_key, extent, deviation, limit, split=(), dtype=jnp.bfloat16):
    gain = block_levels(own_key, extent, split, -0.22, 0.18) if split else 1.0
    values = jax.random.normal(own_key, extent, jnp.float32) * deviation * gain
    return jnp.minimum(jnp.maximum(values, -limit), limit).astype(dtype)


def setup_inputs(seed: int = 0, part: int = 0) -> dict:
    seeds = jax.random.split(jax.random.key(seed), 3)
    part_splits = jax.random.split(jax.random.fold_in(seeds[2], part), 3)
    density_slab = noise(part_splits[0], (AUX, NBF, NBF), (NBF * NBF) ** -0.5, 0.005859375, ((1, 4), (2, 2)))
    orbitals = noise(part_splits[1], (NBF, NPTS), 1.0, 6.0, ((0, 2), (1, 2)))
    return dict(density_slab=density_slab, orbitals=orbitals)


def reference(density_slab, orbitals):
    colloc = orbitals.astype(jnp.float32)

    def one_slice(slab):
        contracted = jnp.dot(slab, orbitals, preferred_element_type=jnp.float32)
        return jnp.sum(colloc * contracted, axis=0)

    weights = lax.map(one_slice, density_slab)
    total = jnp.dot(weights.T, weights, precision=lax.Precision.HIGHEST, preferred_element_type=jnp.float32)
    return total / jnp.float32(AUX)
```

```python
import functools

import jax
import jax.numpy as jnp
from jax import lax
from jax.experimental import pallas as pl
from jax.experimental.pallas import tpu as pltpu
from jax.sharding import PartitionSpec as P

MIB = 1 << 20
ROWS = 256


def weights_kernel(
    tiles, width, block, depth, info, d_hbm, c_hbm, far_hbm, w_ref,
    d_buf, c_buf, p_buf, d_sem, c_sem, p_sem,
):
    core, near, first_row = info[0], info[1], info[2]
    n_groups, rows, _ = d_buf.shape
    span = rows // depth

    def parts(t):
        made = []
        for own, half, start in tiles[t]:
            quarter = core if own else 1 - core
            made.append(pl.multiple_of((quarter * 2 + half) * block + start, 128))
        return made

    def c_copies(t):
        return [
            pltpu.make_async_copy(
                c_hbm.at[:, pl.ds(at, width)], c_buf.at[t % 2, :, pl.ds(i * width, width)], c_sem.at[t % 2]
            )
            for i, at in enumerate(parts(t))
        ]

    def p_start(t):
        for i, at in enumerate(parts(t)):
            to = p_buf.at[t % 2, :, pl.ds(i * width, width)]

            @pl.when(near == 1)
            def _():
                rows_at = pl.ds(pl.multiple_of(first_row, 16), depth)
                pltpu.make_async_copy(c_hbm.at[rows_at, pl.ds(at, width)], to, p_sem.at[t % 2]).start()

            @pl.when(near != 1)
            def _():
                pltpu.make_async_copy(far_hbm.at[:, pl.ds(at, width)], to, p_sem.at[t % 2]).start()

    def p_wait(t):
        for i, at in enumerate(parts(t)):
            to = p_buf.at[t % 2, :, pl.ds(i * width, width)]
            pltpu.make_async_copy(far_hbm.at[:, pl.ds(at, width)], to, p_sem.at[t % 2]).wait()

    def d_copy(g):
        return pltpu.make_async_copy(d_hbm.at[g], d_buf.at[g], d_sem.at[g])

    for copy in c_copies(0):
        copy.start()
    d_copy(0).start()
    p_start(0)
    for g in range(1, n_groups):
        d_copy(g).start()
    for t in range(len(tiles)):
        if t + 1 < len(tiles):
            for copy in c_copies(t + 1):
                copy.start()
            p_start(t + 1)
        for copy in c_copies(t):
            copy.wait()
        if t == 0:
            d_copy(0).wait()
        p_wait(t)
        points = c_buf[t % 2]
        factor = p_buf[t % 2].astype(jnp.float32)
        for g in range(n_groups):
            if t == 0 and g:
                d_copy(g).wait()
            product = jnp.dot(d_buf[g], points, preferred_element_type=jnp.float32)
            summed = jnp.sum(product.reshape(span, depth, -1) * factor[None], axis=1)
            for i in range(len(tiles[t])):
                w_ref[t, i, g * span : (g + 1) * span, :] = summed[:, i * width : (i + 1) * width]


def partial_weights(info, d_rows, orbitals, far, tiles, width, block, depth, n_k):
    q = orbitals.shape[0]
    n_groups = d_rows.shape[0]
    held = len(tiles[0])
    any_space = pl.BlockSpec(memory_space=pl.ANY)
    return pl.pallas_call(
        functools.partial(weights_kernel, tiles, width, block, depth),
        grid_spec=pltpu.PrefetchScalarGridSpec(
            num_scalar_prefetch=1,
            grid=(),
            in_specs=[any_space, any_space, any_space],
            out_specs=pl.BlockSpec(memory_space=pltpu.VMEM),
            scratch_shapes=[
                pltpu.VMEM(d_rows.shape, jnp.bfloat16),
                pltpu.VMEM((2, q, held * width), jnp.bfloat16),
                pltpu.VMEM((2, depth, held * width), jnp.bfloat16),
                pltpu.SemaphoreType.DMA((n_groups,)),
                pltpu.SemaphoreType.DMA((2,)),
                pltpu.SemaphoreType.DMA((2,)),
            ],
        ),
        out_shape=jax.ShapeDtypeStruct((len(tiles), held, n_k, width), jnp.float32),
        compiler_params=pltpu.CompilerParams(vmem_limit_bytes=48 * MIB),
        cost_estimate=pl.CostEstimate(
            flops=2 * n_groups * d_rows.shape[1] * q * len(tiles) * held * width,
            bytes_accessed=2 * (d_rows.size + len(tiles) * held * width * (q + depth)),
            transcendentals=0,
        ),
        name="weights",
    )(info, d_rows, orbitals, far)


def split(x):
    high = x.astype(jnp.bfloat16)
    rest = x - high.astype(jnp.float32)
    middle = rest.astype(jnp.bfloat16)
    low = (rest - middle.astype(jnp.float32)).astype(jnp.bfloat16)
    return high, middle, low


def outer_kernel(scale, n_rows, info, *refs):
    own, other, columns, out = refs[:n_rows], refs[n_rows : 2 * n_rows], refs[2 * n_rows], refs[-1]
    step = pl.program_id(0)

    high, middle, low = split(columns[...] * scale)
    right = jnp.concatenate([high, middle, high, low, middle, high], axis=0)

    def fill(chunks):
        at = 0
        for chunk in chunks:
            high, middle, low = split(chunk[0])
            left = jnp.concatenate([high, high, middle, high, middle, low], axis=0)
            out[at : at + left.shape[1], :] = lax.dot_general(
                left, right, (((0,), (0,)), ((), ())), preferred_element_type=jnp.float32
            )
            at += left.shape[1]

    @pl.when(step < 2)
    def _():
        fill(own)

    @pl.when(step >= 2)
    def _():
        fill(other)


def outer(info, own, other, columns, out_shape, at, before=None):
    n_k, width = columns.shape
    block = out_shape[0] // 4
    row_specs = [
        pl.BlockSpec((1, n_k, x.shape[2]), lambda i, info: (jnp.minimum(i, 1), 0, 0)) for x in own
    ] + [
        pl.BlockSpec((1, n_k, x.shape[2]), lambda i, info: (jnp.maximum(i - 2, 0), 0, 0)) for x in other
    ]
    args = [*own, *other, columns]
    specs = [*row_specs, pl.BlockSpec((n_k, width), lambda i, info: (0, 0))]
    aliases = {}
    if before is not None:
        aliases = {len(args) + 1: 0}
        args.append(before)
        specs.append(pl.BlockSpec(memory_space=pl.ANY))

    def place(i, info):
        quarter = jnp.where(i < 2, info[0], 1 - info[0])
        return quarter * 2 + i % 2, at // width

    return pl.pallas_call(
        functools.partial(outer_kernel, 1.0 / n_k, len(own)),
        grid_spec=pltpu.PrefetchScalarGridSpec(
            num_scalar_prefetch=1,
            grid=(4,),
            in_specs=specs,
            out_specs=pl.BlockSpec((block, width), place),
        ),
        out_shape=jax.ShapeDtypeStruct(out_shape, jnp.float32),
        input_output_aliases=aliases,
        compiler_params=pltpu.CompilerParams(vmem_limit_bytes=48 * MIB),
        cost_estimate=pl.CostEstimate(
            flops=2 * 6 * n_k * out_shape[0] * width, bytes_accessed=4 * out_shape[0] * width, transcendentals=0
        ),
        name="outer",
    )(info, *args)


def swap(x):
    return lax.ppermute(x, "rep", [(0, 1), (1, 0)])


def sum_aux(x, n_aux):
    total = x
    for shift in range(1, n_aux):
        total = total + lax.ppermute(x, "aux", [(i, i ^ shift) for i in range(n_aux)])
    return total


def per_device(n_aux, n_pts, density_slab, orbitals):
    aux, pts, core = lax.axis_index("aux"), lax.axis_index("pts"), lax.axis_index("rep")
    n_k, depth, q = density_slab.shape
    points = orbitals.shape[1]
    block = points // 4
    late = max(block // 4, 128)
    early = block - late
    d_rows = density_slab.reshape(-1, ROWS, q)

    per_core = n_aux // 2
    near = (aux // per_core == core).astype(jnp.int32)
    first_row = (aux % per_core) * depth
    info = jnp.stack([core.astype(jnp.int32), near, first_row.astype(jnp.int32)])
    far = swap(lax.dynamic_slice_in_dim(orbitals, first_row, depth, 0))

    weigh = functools.partial(partial_weights, info, d_rows, orbitals, far, block=block, depth=depth, n_k=n_k)

    def gather(total):
        other = swap(total)
        held = jnp.where(aux % 2 == core, total, other)
        return other, lax.dynamic_index_in_dim(held, core, 0, keepdims=False)

    home = n_aux // n_pts

    def columns_of(held):
        got = held
        for shift in range(1, n_pts):
            pairs = [(a * n_pts + a // home, a * n_pts + (a // home + shift) % n_pts) for a in range(n_aux)]
            came = lax.ppermute(held, ("aux", "pts"), pairs)
            got = jnp.where((pts - aux // home) % n_pts == shift, came, got)
        return got

    a = weigh(tiles=[[(0, 0, 0)], [(0, 1, 0)], [(1, 0, 0)], [(1, 1, 0)]], width=early)[:, 0]
    a_came = swap(a[:2])
    b_send = weigh(tiles=[[(0, 0, early), (0, 1, early)]], width=late)[0]
    a_total = sum_aux(a[2:] + a_came, n_aux)
    b_came = swap(b_send)
    b_keep = weigh(tiles=[[(1, 0, early), (1, 1, early)]], width=late)[0]
    b_total = sum_aux(b_keep + b_came, n_aux)
    a_other, a_held = gather(a_total)
    a_columns = columns_of(a_held)
    b_other, b_held = gather(b_total)
    b_columns = columns_of(b_held)

    out_shape = (points, block)
    own, other = [a_total, b_total], [a_other, b_other]
    first = outer(info, own, other, a_columns, out_shape, 0)
    return outer(info, own, other, b_columns, out_shape, early, first)


def solution(mesh):
    shape = mesh.shape
    return jax.shard_map(
        functools.partial(per_device, shape["aux"], shape["pts"]),
        mesh=mesh,
        in_specs=(P("groups", "aux", "rep"), P(("groups", "rep"), "pts")),
        out_specs=P(("groups", "pts"), ("aux", "rep")),
        check_vma=False,
    )
```

```python
import functools

import jax
import jax.numpy as jnp
from jax import lax
from jax.experimental import pallas as pl
from jax.experimental.pallas import tpu as pltpu
from jax.sharding import PartitionSpec as P

MIB = 1 << 20
ROWS = 256
SLICE_MIB = 50
HEAD_MIB = 36
WEIGHTS_MIB = 32
MADE = 512
PIECES = 2
OUTER_MIB = 40


def slice_kernel(info, c_hbm, first_ref, second_ref, sem):
    depth, points = first_ref.shape
    rows = pl.ds(pl.multiple_of(info[2], 16), depth)
    copies = []
    for i, (quarter, to) in enumerate(((info[0], first_ref), (1 - info[0], second_ref))):
        there = pl.ds(pl.multiple_of(quarter * points, 128), points)
        copies.append(pltpu.make_async_copy(c_hbm.at[rows, there], to, sem.at[i]))
    for copy in copies:
        copy.start()
    for copy in copies:
        copy.wait()


def head_kernel(width, block, info, d_hbm, c_hbm, d_ref, c_ref, *refs):
    products, (d_sem, c_sem) = refs[:-2], refs[-2:]
    piece = width // len(products)
    n_groups = d_ref.shape[0]
    first = pl.multiple_of((1 - info[0]) * 2 * block, 128)

    def c_copy(at, size, i):
        there = pl.ds(at, size)
        return pltpu.make_async_copy(c_hbm.at[:, there], c_ref.at[:, there], c_sem.at[i])

    stages = [0, 1, 4, n_groups]
    d_copies = [
        pltpu.make_async_copy(d_hbm.at[pl.ds(lo, hi - lo)], d_ref.at[pl.ds(lo, hi - lo)], d_sem.at[i])
        for i, (lo, hi) in enumerate(zip(stages, stages[1:]))
    ]
    near = c_copy(first, width, 0)
    rest = [
        c_copy(first + width, 2 * block - width, 1),
        c_copy(pl.multiple_of(info[0] * 2 * block, 128), 2 * block, 2),
    ]
    near.start()
    for copy in d_copies + rest:
        copy.start()
    near.wait()
    for copy, lo, hi in zip(d_copies, stages, stages[1:]):
        copy.wait()
        for g in range(lo, hi):
            product = jnp.dot(d_ref[g], c_ref[:, pl.ds(first, width)], preferred_element_type=jnp.float32)
            for i, ref in enumerate(products):
                ref[g] = product[:, i * piece : (i + 1) * piece]
    for copy in rest:
        copy.wait()


def weights_kernel(tiles, block, depth, info, d_ref, c_ref, far_ref, *refs):
    made, w_ref = refs[:-1], refs[-1]
    core, near, first_row = info[0], info[1], info[2]
    n_groups, rows, _ = d_ref.shape
    span = rows // depth
    origin = min(tile[2] for tile in tiles)
    for t, (own, half, start, width) in enumerate(tiles):
        at = half * block + start
        there = pl.ds(pl.multiple_of((core if own else 1 - core) * 2 * block + at, 128), width)
        mine = c_ref[pl.ds(pl.multiple_of(first_row, 16), depth), there]
        scale = jnp.where(near == 1, mine, far_ref[:, at : at + width]).astype(jnp.float32)
        ready = t - len(tiles) + len(made)
        for g in range(n_groups):
            if ready >= 0:
                product = made[ready][g]
            else:
                product = jnp.dot(d_ref[g], c_ref[:, there], preferred_element_type=jnp.float32)
            w_ref[half, g * span : (g + 1) * span, start - origin : start - origin + width] = jnp.sum(
                product.reshape(span, depth, width) * scale[None], axis=1
            )


VMEM = pl.BlockSpec(memory_space=pltpu.VMEM)
ANY = pl.BlockSpec(memory_space=pl.ANY)


def own_rows(info, orbitals, depth):
    part = jax.ShapeDtypeStruct((depth, orbitals.shape[1] // 2), jnp.bfloat16)
    return pl.pallas_call(
        slice_kernel,
        grid_spec=pltpu.PrefetchScalarGridSpec(
            num_scalar_prefetch=1, grid=(), in_specs=[ANY], out_specs=[VMEM, VMEM],
            scratch_shapes=[pltpu.SemaphoreType.DMA((2,))],
        ),
        out_shape=[part, part],
        compiler_params=pltpu.CompilerParams(vmem_limit_bytes=SLICE_MIB * MIB),
        name="own_rows",
    )(info, orbitals)


def head(info, d_rows, orbitals, width, block):
    n_groups, rows, q = d_rows.shape
    return pl.pallas_call(
        functools.partial(head_kernel, width, block),
        grid_spec=pltpu.PrefetchScalarGridSpec(
            num_scalar_prefetch=1, grid=(), in_specs=[ANY, ANY], out_specs=[VMEM] * (2 + PIECES),
            scratch_shapes=[pltpu.SemaphoreType.DMA((3,)), pltpu.SemaphoreType.DMA((3,))],
        ),
        out_shape=[
            jax.ShapeDtypeStruct(d_rows.shape, jnp.bfloat16),
            jax.ShapeDtypeStruct(orbitals.shape, jnp.bfloat16),
            *[jax.ShapeDtypeStruct((n_groups, rows, width // PIECES), jnp.float32)] * PIECES,
        ],
        compiler_params=pltpu.CompilerParams(vmem_limit_bytes=HEAD_MIB * MIB),
        cost_estimate=pl.CostEstimate(
            flops=2 * n_groups * rows * q * width, bytes_accessed=2 * (d_rows.size + orbitals.size), transcendentals=0
        ),
        name="head",
    )(info, d_rows, orbitals)


def partial_weights(info, d_rows, orbitals, far, made, tiles, width, block, depth, n_k):
    return pl.pallas_call(
        functools.partial(weights_kernel, tiles, block, depth),
        grid_spec=pltpu.PrefetchScalarGridSpec(
            num_scalar_prefetch=1,
            grid=(),
            in_specs=[VMEM] * (3 + len(made)),
            out_specs=VMEM,
        ),
        out_shape=jax.ShapeDtypeStruct((2, n_k, width), jnp.float32),
        compiler_params=pltpu.CompilerParams(vmem_limit_bytes=WEIGHTS_MIB * MIB),
        cost_estimate=pl.CostEstimate(flops=1, bytes_accessed=0, transcendentals=0),
        name="weights",
    )(info, d_rows, orbitals, far, *made)


def split(x):
    high = x.astype(jnp.bfloat16)
    rest = x - high.astype(jnp.float32)
    middle = rest.astype(jnp.bfloat16)
    low = (rest - middle.astype(jnp.float32)).astype(jnp.bfloat16)
    return high, middle, low


def outer_kernel(scale, at, n_rows, info, *refs):
    own, other, columns = refs[:n_rows], refs[n_rows : 2 * n_rows], refs[2 * n_rows]
    out_hbm, buffer, sems = refs[-3:]
    width = columns.shape[1]
    block = sum(x.shape[2] for x in own)

    high, middle, low = split(columns[...] * scale)
    right = jnp.concatenate([high, middle, high, low, middle, high], axis=0)
    copies = []
    row = 0
    for quarter, chunks in ((info[0], own), (1 - info[0], other)):
        for half in range(2):
            start = 0
            for chunk in chunks:
                size = chunk.shape[2]
                step = min(size, 384 if size % 384 == 0 else 256)
                for lo in range(0, size, step):
                    high, middle, low = split(chunk[half, :, lo : lo + step])
                    left = jnp.concatenate([high, high, middle, high, middle, low], axis=0)
                    buffer[row : row + step, :] = lax.dot_general(
                        left, right, (((0,), (0,)), ((), ())), preferred_element_type=jnp.float32
                    )
                    to = pl.multiple_of((quarter * 2 + half) * block + start + lo, 8)
                    copy = pltpu.make_async_copy(
                        buffer.at[pl.ds(row, step)],
                        out_hbm.at[pl.ds(to, step), pl.ds(at, width)],
                        sems.at[len(copies)],
                    )
                    copy.start()
                    copies.append(copy)
                    row += step
                start += size
    for copy in copies:
        copy.wait()


def outer(info, own, other, columns, out_shape, at, before=None):
    n_k, width = columns.shape
    args = [*own, *other, columns]
    specs = [VMEM] * len(args)
    aliases = {}
    if before is not None:
        aliases = {len(args) + 1: 0}
        args.append(before)
        specs.append(ANY)
    return pl.pallas_call(
        functools.partial(outer_kernel, 1.0 / n_k, at, len(own)),
        grid_spec=pltpu.PrefetchScalarGridSpec(
            num_scalar_prefetch=1,
            grid=(),
            in_specs=specs,
            out_specs=ANY,
            scratch_shapes=[pltpu.VMEM((out_shape[0], width), jnp.float32), pltpu.SemaphoreType.DMA((32,))],
        ),
        out_shape=jax.ShapeDtypeStruct(out_shape, jnp.float32),
        input_output_aliases=aliases,
        compiler_params=pltpu.CompilerParams(vmem_limit_bytes=OUTER_MIB * MIB),
        cost_estimate=pl.CostEstimate(
            flops=2 * 6 * n_k * out_shape[0] * width, bytes_accessed=4 * out_shape[0] * width, transcendentals=0
        ),
        name="outer",
    )(info, *args)


def swap(x):
    return lax.ppermute(x, "rep", [(0, 1), (1, 0)])


def sum_aux(x, n_aux):
    total = x
    for shift in range(1, n_aux):
        total = total + lax.ppermute(x, "aux", [(i, i ^ shift) for i in range(n_aux)])
    return total


def per_device(n_aux, n_pts, density_slab, orbitals):
    aux, pts, core = lax.axis_index("aux"), lax.axis_index("pts"), lax.axis_index("rep")
    n_k, depth, q = density_slab.shape
    points = orbitals.shape[1]
    block = points // 4
    late = max(block // 4, 128)
    early = block - late
    d_rows = density_slab.reshape(-1, ROWS, q)

    per_core = n_aux // 2
    near = (aux // per_core == core).astype(jnp.int32)
    first_row = (aux % per_core) * depth
    info = jnp.stack([core.astype(jnp.int32), near, first_row.astype(jnp.int32)])
    far = [swap(part) for part in own_rows(info, orbitals, depth)]

    ahead = min(early, MADE)
    d_near, c_near, *made = head(info, d_rows, orbitals, ahead, block)

    def weigh(own, width, start, made=(), after=None):
        order = info if after is None else lax.optimization_barrier((info, after))[0]
        tiles = [(own, half, start, width) for half in range(2)]
        if made:
            tiles = [(own, 1, start, width), (own, 0, ahead, width - ahead)]
            tiles += [(own, 0, i * ahead // PIECES, ahead // PIECES) for i in range(PIECES)]
            tiles = [tile for tile in tiles if tile[3]]
        return partial_weights(order, d_near, c_near, far[own], made, tiles, width, block, depth, n_k)

    def gather(total):
        other = swap(total)
        held = jnp.where(aux % 2 == core, total, other)
        return other, lax.dynamic_index_in_dim(held, core, 0, keepdims=False)

    home = n_aux // n_pts

    def columns_of(held):
        got = held
        for shift in range(1, n_pts):
            came = lax.ppermute(held, "pts", [(i, (i + shift) % n_pts) for i in range(n_pts)])
            got = jnp.where((pts - aux // home) % n_pts == shift, came, got)
        return got

    a_send = weigh(0, early, 0, made)
    a_came = swap(a_send)
    a_keep = weigh(1, early, 0, after=a_send)
    a_total = sum_aux(a_keep + a_came, n_aux)
    b_send = weigh(0, late, early, after=a_keep)
    b_came = swap(b_send)
    b_keep = weigh(1, late, early, after=b_send)
    b_partial, a_total = lax.optimization_barrier((b_keep + b_came, a_total))
    a_other, a_held = gather(a_total)
    b_total, a_other, a_columns = lax.optimization_barrier((sum_aux(b_partial, n_aux), a_other, columns_of(a_held)))
    b_other, b_held = gather(b_total)
    b_columns = columns_of(b_held)

    out_shape = (points, block)
    own, other = [a_total, b_total], [a_other, b_other]
    first = outer(info, own, other, a_columns, out_shape, 0)
    return outer(info, own, other, b_columns, out_shape, early, first)


def solution(mesh):
    shape = mesh.shape
    return jax.shard_map(
        functools.partial(per_device, shape["aux"], shape["pts"]),
        mesh=mesh,
        in_specs=(P("groups", "aux", "rep"), P(("groups", "rep"), "pts")),
        out_specs=P(("groups", "pts"), ("aux", "rep")),
        check_vma=False,
    )
```

```python
import functools

import jax
import jax.numpy as jnp
from jax import lax
from jax.experimental import pallas as pl
from jax.experimental.pallas import tpu as pltpu
from jax.sharding import PartitionSpec as P

MIB = 1 << 20
ROWS = 256
SLICE_MIB = 50
LOAD_MIB = 44
WEIGHTS_MIB = 36
OUTER_MIB = 40
TILE = 512


def first_kernel(c_hbm, rows_ref, sem):
    depth, points = rows_ref.shape
    place = Place(depth, points)
    copy = pltpu.make_async_copy(c_hbm.at[place.rows, place.quarter(1)], rows_ref, sem)
    copy.start()
    copy.wait()


def load_kernel(c_hbm, sent, c_ref, next_ref, rows_ref, sems):
    depth, points = rows_ref.shape
    place = Place(depth, points)
    copies = [
        pltpu.make_async_copy(c_hbm.at[place.rows, place.quarter(0)], rows_ref, sems.at[0]),
        pltpu.make_async_copy(c_hbm.at[:, place.quarter(0)], c_ref, sems.at[1]),
        pltpu.make_async_copy(c_hbm.at[:, place.quarter(1)], next_ref, sems.at[2]),
    ]
    for copy in copies:
        copy.start()
    for copy in copies:
        copy.wait()


class Place:
    def __init__(self, depth, points):
        self.core = lax.axis_index("rep")
        aux = lax.axis_index("aux")
        per_core = lax.axis_size("aux") // 2
        self.near = aux // per_core == self.core
        self.rows = pl.ds(pl.multiple_of(aux % per_core * depth, 16), depth)
        self.points = points

    def quarter(self, own):
        return pl.ds(pl.multiple_of((self.core if own else 1 - self.core) * self.points, 128), self.points)


def weights_kernel(own, chunks, tile, depth, d_ref, c_ref, far_ref, *refs):
    n_groups, rows, _ = d_ref.shape
    span = rows // depth
    points = c_ref.shape[1]
    block = points // 2
    place = Place(depth, points)
    outs = refs
    for (start, width), w_ref in zip(chunks, outs):
        for half in range(2):
            for lo in range(0, width, tile):
                size = min(tile, width - lo)
                there = slice(half * block + start + lo, half * block + start + lo + size)
                scale = jnp.where(place.near, c_ref[place.rows, there], far_ref[:, there]).astype(jnp.float32)
                for g in range(n_groups):
                    product = jnp.dot(d_ref[g], c_ref[:, there], preferred_element_type=jnp.float32)
                    w_ref[half, g * span : (g + 1) * span, lo : lo + size] = jnp.sum(
                        product.reshape(span, depth, size) * scale[None], axis=1
                    )


VMEM = pl.BlockSpec(memory_space=pltpu.VMEM)
ANY = pl.BlockSpec(memory_space=pl.ANY)


def limit(mib):
    return pltpu.CompilerParams(vmem_limit_bytes=mib * MIB)


def first_rows(orbitals, depth):
    return pl.pallas_call(
        first_kernel,
        in_specs=[ANY],
        out_specs=VMEM,
        scratch_shapes=[pltpu.SemaphoreType.DMA],
        out_shape=jax.ShapeDtypeStruct((depth, orbitals.shape[1] // 2), jnp.bfloat16),
        compiler_params=limit(SLICE_MIB),
        name="first_rows",
    )(orbitals)


def load(orbitals, sent, depth):
    q, points = orbitals.shape
    part = jax.ShapeDtypeStruct((q, points // 2), jnp.bfloat16)
    return pl.pallas_call(
        load_kernel,
        in_specs=[ANY, ANY],
        out_specs=[VMEM] * 3,
        scratch_shapes=[pltpu.SemaphoreType.DMA((3,))],
        out_shape=[part, part, jax.ShapeDtypeStruct((depth, points // 2), jnp.bfloat16)],
        compiler_params=limit(LOAD_MIB),
        cost_estimate=pl.CostEstimate(flops=0, bytes_accessed=2 * orbitals.size, transcendentals=0),
        name="load",
    )(orbitals, sent)


def quarter_weights(own, chunks, depth, n_k, d_rows, c_part, far, *more):
    outs = [jax.ShapeDtypeStruct((2, n_k, width), jnp.float32) for _, width in chunks]
    return pl.pallas_call(
        functools.partial(weights_kernel, own, chunks, TILE, depth),
        in_specs=[VMEM] * 3 + [ANY] * len(more),
        out_specs=[VMEM] * len(outs),
        scratch_shapes=[],
        out_shape=outs,
        compiler_params=limit(WEIGHTS_MIB),
        cost_estimate=pl.CostEstimate(
            flops=2 * d_rows.size * c_part.shape[1], bytes_accessed=0, transcendentals=0
        ),
        name="weights",
    )(d_rows, c_part, far, *more)


def split(x):
    high = x.astype(jnp.bfloat16)
    rest = x - high.astype(jnp.float32)
    middle = rest.astype(jnp.bfloat16)
    low = (rest - middle.astype(jnp.float32)).astype(jnp.bfloat16)
    return high, middle, low


def outer_kernel(scale, at, n_rows, *refs):
    own, other, columns = refs[:n_rows], refs[n_rows : 2 * n_rows], refs[2 * n_rows]
    out_hbm, buffer, sems = refs[-3:]
    width = columns.shape[1]
    block = sum(x.shape[2] for x in own)

    high, middle, low = split(columns[...] * scale)
    right = jnp.concatenate([high, middle, high, low, middle, high], axis=0)
    copies = []
    row = 0
    core = lax.axis_index("rep")
    for quarter, chunks in ((core, own), (1 - core, other)):
        for half in range(2):
            start = 0
            for chunk in chunks:
                size = chunk.shape[2]
                step = min(size, 384 if size % 384 == 0 else 256)
                for lo in range(0, size, step):
                    high, middle, low = split(chunk[half, :, lo : lo + step])
                    left = jnp.concatenate([high, high, middle, high, middle, low], axis=0)
                    buffer[row : row + step, :] = lax.dot_general(
                        left, right, (((0,), (0,)), ((), ())), preferred_element_type=jnp.float32
                    )
                    to = pl.multiple_of((quarter * 2 + half) * block + start + lo, 8)
                    copy = pltpu.make_async_copy(
                        buffer.at[pl.ds(row, step)],
                        out_hbm.at[pl.ds(to, step), pl.ds(at, width)],
                        sems.at[len(copies)],
                    )
                    copy.start()
                    copies.append(copy)
                    row += step
                start += size
    for copy in copies:
        copy.wait()


def outer(own, other, columns, out_shape, at, before=None):
    n_k, width = columns.shape
    args = [*own, *other, columns]
    specs = [VMEM] * len(args)
    aliases = {}
    if before is not None:
        aliases = {len(args): 0}
        args.append(before)
        specs.append(ANY)
    return pl.pallas_call(
        functools.partial(outer_kernel, 1.0 / n_k, at, len(own)),
        in_specs=specs,
        out_specs=ANY,
        scratch_shapes=[pltpu.VMEM((out_shape[0], width), jnp.float32), pltpu.SemaphoreType.DMA((32,))],
        out_shape=jax.ShapeDtypeStruct(out_shape, jnp.float32),
        input_output_aliases=aliases,
        compiler_params=limit(OUTER_MIB),
        cost_estimate=pl.CostEstimate(
            flops=2 * 6 * n_k * out_shape[0] * width, bytes_accessed=4 * out_shape[0] * width, transcendentals=0
        ),
        name="outer",
    )(*args)


def swap(x):
    return lax.ppermute(x, "rep", [(0, 1), (1, 0)])


def sum_aux(x, n_aux):
    total = x
    for shift in range(n_aux - 1, 0, -1):
        total = total + lax.ppermute(x, "aux", [(i, i ^ shift) for i in range(n_aux)])
    return total


def per_device(n_aux, n_pts, density_slab, orbitals):
    aux, pts, core = lax.axis_index("aux"), lax.axis_index("pts"), lax.axis_index("rep")
    n_k, depth, q = density_slab.shape
    points = orbitals.shape[1]
    block = points // 4
    chunks = [(0, block)]
    d_rows = density_slab.reshape(-1, ROWS, q)

    sent = first_rows(orbitals, depth)
    far_first = swap(sent)
    c_first, c_second, sent = load(orbitals, sent, depth)
    far_second = swap(sent)
    sends = quarter_weights(False, chunks, depth, n_k, d_rows, c_first, far_first)
    came = [swap(x) for x in sends]
    keeps = quarter_weights(True, chunks, depth, n_k, d_rows, c_second, far_second)
    total = sum_aux(keeps[0] + came[0], n_aux)

    def gather(total):
        other = swap(total)
        held = jnp.where(aux % 2 == core, total, other)
        return other, lax.dynamic_index_in_dim(held, core, 0, keepdims=False)

    home = n_aux // n_pts

    def columns_of(held):
        got = held
        for shift in range(1, n_pts):
            came = lax.ppermute(held, "pts", [(i, (i + shift) % n_pts) for i in range(n_pts)])
            got = jnp.where((pts - aux // home) % n_pts == shift, came, got)
        return got

    other, held = gather(total)
    return outer([total], [other], columns_of(held), (points, block), 0)


def solution(mesh):
    shape = mesh.shape
    return jax.shard_map(
        functools.partial(per_device, shape["aux"], shape["pts"]),
        mesh=mesh,
        in_specs=(P("groups", "aux", "rep"), P(("groups", "rep"), "pts")),
        out_specs=P(("groups", "pts"), ("aux", "rep")),
        check_vma=False,
    )
```

```python
import functools

import jax
import jax.numpy as jnp
from jax import lax
from jax.experimental import pallas as pl
from jax.experimental.pallas import tpu as pltpu
from jax.sharding import PartitionSpec as P

MIB = 1 << 20
ROWS = 256
SLICE_MIB = 50
LOAD_MIB = 44
WEIGHTS_MIB = 36
OUTER_MIB = 40
TILE = 512


def first_kernel(c_hbm, rows_ref, sems):
    depth, points = rows_ref.shape
    place = Place(depth, points)
    copies = place.copies(1, c_hbm.at[place.rows], rows_ref, sems)
    for copy in copies:
        copy.start()
    for copy in copies:
        copy.wait()


def load_kernel(c_hbm, sent, c_ref, next_ref, rows_ref, sems):
    depth, points = rows_ref.shape
    place = Place(depth, points)
    first = place.copies(0, c_hbm, c_ref, sems.at[pl.ds(0, 2)])
    second = place.copies(1, c_hbm, next_ref, sems.at[pl.ds(2, 2)])
    rows = pltpu.make_async_copy(c_ref.at[place.rows], rows_ref, sems.at[4])
    for copy in first + second:
        copy.start()
    for copy in first:
        copy.wait()
    rows.start()
    for copy in second:
        copy.wait()
    rows.wait()


class Place:
    def __init__(self, depth, points):
        self.core = lax.axis_index("rep")
        aux = lax.axis_index("aux")
        per_core = lax.axis_size("aux") // 2
        self.near = aux // per_core == self.core
        self.rows = pl.ds(pl.multiple_of(aux % per_core * depth, 16), depth)
        self.block = points // 2

    def copies(self, own, source, target, sems):
        core = self.core if own else 1 - self.core
        return [
            pltpu.make_async_copy(
                source.at[:, pl.ds(pl.multiple_of((2 * i + core) * self.block, 128), self.block)],
                target.at[:, pl.ds(i * self.block, self.block)],
                sems.at[i],
            )
            for i in range(2)
        ]


def weights_kernel(own, chunks, tile, depth, d_ref, c_ref, far_ref, *refs):
    n_groups, rows, _ = d_ref.shape
    span = rows // depth
    points = c_ref.shape[1]
    block = points // 2
    place = Place(depth, points)
    outs = refs
    for (start, width), w_ref in zip(chunks, outs):
        for half in range(2):
            for lo in range(0, width, tile):
                size = min(tile, width - lo)
                there = slice(half * block + start + lo, half * block + start + lo + size)
                scale = jnp.where(place.near, c_ref[place.rows, there], far_ref[:, there]).astype(jnp.float32)
                for g in range(n_groups):
                    product = jnp.dot(d_ref[g], c_ref[:, there], preferred_element_type=jnp.float32)
                    w_ref[half, g * span : (g + 1) * span, lo : lo + size] = jnp.sum(
                        product.reshape(span, depth, size) * scale[None], axis=1
                    )


VMEM = pl.BlockSpec(memory_space=pltpu.VMEM)
ANY = pl.BlockSpec(memory_space=pl.ANY)


def limit(mib):
    return pltpu.CompilerParams(vmem_limit_bytes=mib * MIB)


def first_rows(orbitals, depth):
    return pl.pallas_call(
        first_kernel,
        in_specs=[ANY],
        out_specs=VMEM,
        scratch_shapes=[pltpu.SemaphoreType.DMA((2,))],
        out_shape=jax.ShapeDtypeStruct((depth, orbitals.shape[1] // 2), jnp.bfloat16),
        compiler_params=limit(SLICE_MIB),
        name="first_rows",
    )(orbitals)


def load(orbitals, sent, depth):
    q, points = orbitals.shape
    part = jax.ShapeDtypeStruct((q, points // 2), jnp.bfloat16)
    return pl.pallas_call(
        load_kernel,
        in_specs=[ANY, ANY],
        out_specs=[VMEM] * 3,
        scratch_shapes=[pltpu.SemaphoreType.DMA((5,))],
        out_shape=[part, part, jax.ShapeDtypeStruct((depth, points // 2), jnp.bfloat16)],
        compiler_params=limit(LOAD_MIB),
        cost_estimate=pl.CostEstimate(flops=0, bytes_accessed=2 * orbitals.size, transcendentals=0),
        name="load",
    )(orbitals, sent)


def quarter_weights(own, chunks, depth, n_k, d_rows, c_part, far, *more):
    outs = [jax.ShapeDtypeStruct((2, n_k, width), jnp.float32) for _, width in chunks]
    return pl.pallas_call(
        functools.partial(weights_kernel, own, chunks, TILE, depth),
        in_specs=[VMEM] * 3 + [ANY] * len(more),
        out_specs=[VMEM] * len(outs),
        scratch_shapes=[],
        out_shape=outs,
        compiler_params=limit(WEIGHTS_MIB),
        cost_estimate=pl.CostEstimate(
            flops=2 * d_rows.size * c_part.shape[1], bytes_accessed=0, transcendentals=0
        ),
        name="weights",
    )(d_rows, c_part, far, *more)


def split(x):
    high = x.astype(jnp.bfloat16)
    rest = x - high.astype(jnp.float32)
    middle = rest.astype(jnp.bfloat16)
    low = (rest - middle.astype(jnp.float32)).astype(jnp.bfloat16)
    return high, middle, low


def outer_kernel(scale, at, n_rows, *refs):
    own, other, columns = refs[:n_rows], refs[n_rows : 2 * n_rows], refs[2 * n_rows]
    out_hbm, buffer, sems = refs[-3:]
    width = columns.shape[1]
    block = sum(x.shape[2] for x in own)

    high, middle, low = split(columns[...] * scale)
    right = jnp.concatenate([high, middle, high, low, middle, high], axis=0)
    copies = []
    row = 0
    core = lax.axis_index("rep")
    for side, chunks in ((core, own), (1 - core, other)):
        for half in range(2):
            start = 0
            for chunk in chunks:
                size = chunk.shape[2]
                step = min(size, 384 if size % 384 == 0 else 256)
                for lo in range(0, size, step):
                    high, middle, low = split(chunk[half, :, lo : lo + step])
                    left = jnp.concatenate([high, high, middle, high, middle, low], axis=0)
                    buffer[row : row + step, :] = lax.dot_general(
                        left, right, (((0,), (0,)), ((), ())), preferred_element_type=jnp.float32
                    )
                    to = pl.multiple_of((half * 2 + side) * block + start + lo, 8)
                    copy = pltpu.make_async_copy(
                        buffer.at[pl.ds(row, step)],
                        out_hbm.at[pl.ds(to, step), pl.ds(at, width)],
                        sems.at[len(copies)],
                    )
                    copy.start()
                    copies.append(copy)
                    row += step
                start += size
    for copy in copies:
        copy.wait()


def outer(own, other, columns, out_shape, at, before=None):
    n_k, width = columns.shape
    args = [*own, *other, columns]
    specs = [VMEM] * len(args)
    aliases = {}
    if before is not None:
        aliases = {len(args): 0}
        args.append(before)
        specs.append(ANY)
    return pl.pallas_call(
        functools.partial(outer_kernel, 1.0 / n_k, at, len(own)),
        in_specs=specs,
        out_specs=ANY,
        scratch_shapes=[pltpu.VMEM((out_shape[0], width), jnp.float32), pltpu.SemaphoreType.DMA((32,))],
        out_shape=jax.ShapeDtypeStruct(out_shape, jnp.float32),
        input_output_aliases=aliases,
        compiler_params=limit(OUTER_MIB),
        cost_estimate=pl.CostEstimate(
            flops=2 * 6 * n_k * out_shape[0] * width, bytes_accessed=4 * out_shape[0] * width, transcendentals=0
        ),
        name="outer",
    )(*args)


def swap(x):
    return lax.ppermute(x, "rep", [(0, 1), (1, 0)])


def sum_aux(x, n_aux):
    total = x
    middle = n_aux // 2
    for shift in [i for i in range(1, n_aux) if i != middle] + [middle]:
        total = total + lax.ppermute(x, "aux", [(i, i ^ shift) for i in range(n_aux)])
    return total


def per_device(n_aux, n_pts, density_slab, orbitals):
    aux, pts = lax.axis_index("aux"), lax.axis_index("pts")
    n_k, depth, q = density_slab.shape
    points = orbitals.shape[1]
    block = points // 4
    chunks = [(0, block)]
    d_rows = density_slab.reshape(-1, ROWS, q)

    sent = first_rows(orbitals, depth)
    far_first = swap(sent)
    c_first, c_second, sent = load(orbitals, sent, depth)
    far_second = swap(sent)
    sends = quarter_weights(False, chunks, depth, n_k, d_rows, c_first, far_first)
    came = [swap(x) for x in sends]
    keeps = quarter_weights(True, chunks, depth, n_k, d_rows, c_second, far_second)
    total = sum_aux(keeps[0] + came[0], n_aux)

    home = n_aux // n_pts

    def columns_of(held):
        got = held
        for shift in range(1, n_pts):
            came = lax.ppermute(held, "pts", [(i, (i + shift) % n_pts) for i in range(n_pts)])
            got = jnp.where((pts - aux // home) % n_pts == shift, came, got)
        return got

    held = lax.dynamic_index_in_dim(total, aux % 2, 0, keepdims=False)
    return outer([total], [swap(total)], columns_of(held), (points, block), 0)


def solution(mesh):
    shape = mesh.shape
    return jax.shard_map(
        functools.partial(per_device, shape["aux"], shape["pts"]),
        mesh=mesh,
        in_specs=(P("groups", "aux", "rep"), P(("groups", "rep"), "pts")),
        out_specs=P(("groups", "pts"), ("aux", "rep")),
        check_vma=False,
    )
```

```python
import functools

import jax
import jax.numpy as jnp
from jax import lax
from jax.experimental import pallas as pl
from jax.experimental.pallas import tpu as pltpu
from jax.sharding import PartitionSpec as P

MIB = 1 << 20
ROWS = 256
SLICE_MIB = 50
LOAD_MIB = 44
WEIGHTS_MIB = 36
OUTER_MIB = 40
TILE = 512


def first_kernel(c_hbm, rows_ref, sems):
    depth, points = rows_ref.shape
    place = Place(depth, points)
    copies = place.copies(1, c_hbm.at[place.rows], rows_ref, sems)
    for copy in copies:
        copy.start()
    for copy in copies:
        copy.wait()


def load_kernel(c_hbm, sent, c_ref, next_ref, rows_ref, sems):
    depth, points = rows_ref.shape
    place = Place(depth, points)
    first = place.copies(0, c_hbm, c_ref, sems.at[pl.ds(0, 2)])
    second = place.copies(1, c_hbm, next_ref, sems.at[pl.ds(2, 2)])
    rows = pltpu.make_async_copy(c_ref.at[place.rows], rows_ref, sems.at[4])
    for copy in first + second:
        copy.start()
    for copy in first:
        copy.wait()
    rows.start()
    for copy in second:
        copy.wait()
    rows.wait()


class Place:
    def __init__(self, depth, points):
        self.core = lax.axis_index("rep")
        aux = lax.axis_index("aux")
        per_core = lax.axis_size("aux") // 2
        self.near = aux // per_core == self.core
        self.rows = pl.ds(pl.multiple_of(aux % per_core * depth, 16), depth)
        self.parity = aux % 2
        self.block = points // 2

    def copies(self, own, source, target, sems):
        core = self.core if own else 1 - self.core
        return [
            pltpu.make_async_copy(
                source.at[:, pl.ds(pl.multiple_of(((i + self.parity) % 2 * 2 + core) * self.block, 128), self.block)],
                target.at[:, pl.ds(i * self.block, self.block)],
                sems.at[i],
            )
            for i in range(2)
        ]


def weights_kernel(own, chunks, tile, depth, d_ref, c_ref, far_ref, *refs):
    n_groups, rows, _ = d_ref.shape
    span = rows // depth
    points = c_ref.shape[1]
    block = points // 2
    place = Place(depth, points)
    for half, w_ref in enumerate(refs):
        for start, width in chunks:
            for lo in range(0, width, tile):
                size = min(tile, width - lo)
                there = slice(half * block + start + lo, half * block + start + lo + size)
                scale = jnp.where(place.near, c_ref[place.rows, there], far_ref[:, there]).astype(jnp.float32)
                for g in range(n_groups):
                    product = jnp.dot(d_ref[g], c_ref[:, there], preferred_element_type=jnp.float32)
                    w_ref[g * span : (g + 1) * span, lo : lo + size] = jnp.sum(
                        product.reshape(span, depth, size) * scale[None], axis=1
                    )


VMEM = pl.BlockSpec(memory_space=pltpu.VMEM)
ANY = pl.BlockSpec(memory_space=pl.ANY)


def limit(mib):
    return pltpu.CompilerParams(vmem_limit_bytes=mib * MIB)


def first_rows(orbitals, depth):
    return pl.pallas_call(
        first_kernel,
        in_specs=[ANY],
        out_specs=VMEM,
        scratch_shapes=[pltpu.SemaphoreType.DMA((2,))],
        out_shape=jax.ShapeDtypeStruct((depth, orbitals.shape[1] // 2), jnp.bfloat16),
        compiler_params=limit(SLICE_MIB),
        name="first_rows",
    )(orbitals)


def load(orbitals, sent, depth):
    q, points = orbitals.shape
    part = jax.ShapeDtypeStruct((q, points // 2), jnp.bfloat16)
    return pl.pallas_call(
        load_kernel,
        in_specs=[ANY, ANY],
        out_specs=[VMEM] * 3,
        scratch_shapes=[pltpu.SemaphoreType.DMA((5,))],
        out_shape=[part, part, jax.ShapeDtypeStruct((depth, points // 2), jnp.bfloat16)],
        compiler_params=limit(LOAD_MIB),
        cost_estimate=pl.CostEstimate(flops=0, bytes_accessed=2 * orbitals.size, transcendentals=0),
        name="load",
    )(orbitals, sent)


def quarter_weights(own, chunks, depth, n_k, d_rows, c_part, far, *more):
    outs = [jax.ShapeDtypeStruct((n_k, c_part.shape[1] // 2), jnp.float32)] * 2
    return pl.pallas_call(
        functools.partial(weights_kernel, own, chunks, TILE, depth),
        in_specs=[VMEM] * 3 + [ANY] * len(more),
        out_specs=[VMEM] * len(outs),
        scratch_shapes=[],
        out_shape=outs,
        compiler_params=limit(WEIGHTS_MIB),
        cost_estimate=pl.CostEstimate(
            flops=2 * d_rows.size * c_part.shape[1], bytes_accessed=0, transcendentals=0
        ),
        name="weights",
    )(d_rows, c_part, far, *more)


def split(x):
    high = x.astype(jnp.bfloat16)
    rest = x - high.astype(jnp.float32)
    middle = rest.astype(jnp.bfloat16)
    low = (rest - middle.astype(jnp.float32)).astype(jnp.bfloat16)
    return high, middle, low


def outer_kernel(scale, *refs):
    *rows, columns, out_hbm, buffer, sems = refs
    core, parity = lax.axis_index("rep"), lax.axis_index("aux") % 2
    high, middle, low = split(columns[...] * scale)
    right = jnp.concatenate([high, middle, high, low, middle, high], axis=0)
    copies = []
    for i, weights in enumerate(rows):
        block = weights.shape[1]
        half = 1 - parity if i % 2 else parity
        side = 1 - core if i // 2 else core
        step = min(block, ROWS)
        for lo in range(0, block, step):
            high, middle, low = split(weights[:, lo : lo + step])
            left = jnp.concatenate([high, high, middle, high, middle, low], axis=0)
            here = pl.ds(i * block + lo, step)
            buffer[here, :] = lax.dot_general(
                left, right, (((0,), (0,)), ((), ())), preferred_element_type=jnp.float32
            )
            to = pl.ds(pl.multiple_of((half * 2 + side) * block + lo, 8), step)
            copy = pltpu.make_async_copy(buffer.at[here], out_hbm.at[to], sems.at[len(copies)])
            copy.start()
            copies.append(copy)
    for copy in copies:
        copy.wait()


def outer(rows, columns, out_shape):
    n_k, width = columns.shape
    return pl.pallas_call(
        functools.partial(outer_kernel, 1.0 / n_k),
        in_specs=[VMEM] * (len(rows) + 1),
        out_specs=ANY,
        scratch_shapes=[pltpu.VMEM(out_shape, jnp.float32), pltpu.SemaphoreType.DMA((32,))],
        out_shape=jax.ShapeDtypeStruct(out_shape, jnp.float32),
        compiler_params=limit(OUTER_MIB),
        cost_estimate=pl.CostEstimate(
            flops=2 * 6 * n_k * out_shape[0] * width, bytes_accessed=4 * out_shape[0] * width, transcendentals=0
        ),
        name="outer",
    )(*rows, columns)


def swap(x):
    return lax.ppermute(x, "rep", [(0, 1), (1, 0)])


def from_aux(even, odd, n_aux):
    middle = n_aux // 2
    return [
        lax.ppermute(odd if shift % 2 else even, "aux", [(i, i ^ shift) for i in range(n_aux)])
        for shift in [middle] + [i for i in range(1, n_aux) if i != middle]
    ]


def per_device(n_aux, n_pts, density_slab, orbitals):
    aux, pts = lax.axis_index("aux"), lax.axis_index("pts")
    n_k, depth, q = density_slab.shape
    points = orbitals.shape[1]
    block = points // 4
    chunks = [(0, block)]
    d_rows = density_slab.reshape(-1, ROWS, q)

    sent = first_rows(orbitals, depth)
    far_first = swap(sent)
    c_first, c_second, sent = load(orbitals, sent, depth)
    far_second = swap(sent)
    sends = quarter_weights(False, chunks, depth, n_k, d_rows, c_first, far_first)
    came = [swap(x) for x in sends]
    keeps = quarter_weights(True, chunks, depth, n_k, d_rows, c_second, far_second)
    mine, cross = lax.optimization_barrier([x + y for x, y in zip(keeps, came)])

    a_came = from_aux(mine, cross, n_aux)
    b_came = from_aux(cross, mine, n_aux)
    a_total = sum(a_came, mine)

    home = n_aux // n_pts

    def columns_of(held):
        got = held
        for shift in range(1, n_pts):
            came = lax.ppermute(held, "pts", [(i, (i + shift) % n_pts) for i in range(n_pts)])
            got = jnp.where((pts - aux // home) % n_pts == shift, came, got)
        return got

    columns = columns_of(a_total)
    b_total = sum(b_came, cross)
    rows = [a_total, b_total, swap(a_total), swap(b_total)]
    return outer(rows, columns, (points, block))


def solution(mesh):
    shape = mesh.shape
    return jax.shard_map(
        functools.partial(per_device, shape["aux"], shape["pts"]),
        mesh=mesh,
        in_specs=(P("groups", "aux", "rep"), P(("groups", "rep"), "pts")),
        out_specs=P(("groups", "pts"), ("aux", "rep")),
        check_vma=False,
    )
```

```python
import functools

import jax
import jax.numpy as jnp
from jax import lax
from jax.experimental import pallas as pl
from jax.experimental.pallas import tpu as pltpu
from jax.sharding import PartitionSpec as P

MIB = 1 << 20
ROWS = 256
SLICE_MIB = 50
LOAD_MIB = 44
WEIGHTS_MIB = 36
OUTER_MIB = 40
TILE = 512


def first_kernel(c_hbm, rows_ref, sems):
    depth, points = rows_ref.shape
    place = Place(depth, points)
    copies = place.copies(1, c_hbm.at[place.rows], rows_ref, sems)
    for copy in copies:
        copy.start()
    for copy in copies:
        copy.wait()


def load_kernel(c_hbm, sent, c_ref, next_ref, rows_ref, sems):
    depth, points = rows_ref.shape
    place = Place(depth, points)
    first = place.copies(0, c_hbm, c_ref, sems.at[pl.ds(0, 2)])
    second = place.copies(1, c_hbm, next_ref, sems.at[pl.ds(2, 2)])
    rows = pltpu.make_async_copy(c_ref.at[place.rows], rows_ref, sems.at[4])
    for copy in first + second:
        copy.start()
    for copy in first:
        copy.wait()
    rows.start()
    for copy in second:
        copy.wait()
    rows.wait()


class Place:
    def __init__(self, depth, points):
        self.core = lax.axis_index("rep")
        aux = lax.axis_index("aux")
        per_core = lax.axis_size("aux") // 2
        self.near = aux // per_core == self.core
        self.rows = pl.ds(pl.multiple_of(aux % per_core * depth, 16), depth)
        self.parity = aux % 2
        self.block = points // 2

    def copies(self, own, source, target, sems):
        core = self.core if own else 1 - self.core
        return [
            pltpu.make_async_copy(
                source.at[:, pl.ds(pl.multiple_of(((i + self.parity) % 2 * 2 + core) * self.block, 128), self.block)],
                target.at[:, pl.ds(i * self.block, self.block)],
                sems.at[i],
            )
            for i in range(2)
        ]


def weights_kernel(own, chunks, tile, depth, d_ref, c_ref, far_ref, *refs):
    n_groups, rows, _ = d_ref.shape
    span = rows // depth
    points = c_ref.shape[1]
    block = points // 2
    place = Place(depth, points)
    for half, w_ref in enumerate(refs):
        for start, width in chunks:
            for lo in range(0, width, tile):
                size = min(tile, width - lo)
                there = slice(half * block + start + lo, half * block + start + lo + size)
                scale = jnp.where(place.near, c_ref[place.rows, there], far_ref[:, there]).astype(jnp.float32)
                for g in range(n_groups):
                    product = jnp.dot(d_ref[g], c_ref[:, there], preferred_element_type=jnp.float32)
                    w_ref[g * span : (g + 1) * span, lo : lo + size] = jnp.sum(
                        product.reshape(span, depth, size) * scale[None], axis=1
                    )


VMEM = pl.BlockSpec(memory_space=pltpu.VMEM)
ANY = pl.BlockSpec(memory_space=pl.ANY)


def limit(mib):
    return pltpu.CompilerParams(vmem_limit_bytes=mib * MIB)


def first_rows(orbitals, depth):
    return pl.pallas_call(
        first_kernel,
        in_specs=[ANY],
        out_specs=VMEM,
        scratch_shapes=[pltpu.SemaphoreType.DMA((2,))],
        out_shape=jax.ShapeDtypeStruct((depth, orbitals.shape[1] // 2), jnp.bfloat16),
        compiler_params=limit(SLICE_MIB),
        name="first_rows",
    )(orbitals)


def load(orbitals, sent, depth):
    q, points = orbitals.shape
    part = jax.ShapeDtypeStruct((q, points // 2), jnp.bfloat16)
    return pl.pallas_call(
        load_kernel,
        in_specs=[ANY, ANY],
        out_specs=[VMEM] * 3,
        scratch_shapes=[pltpu.SemaphoreType.DMA((5,))],
        out_shape=[part, part, jax.ShapeDtypeStruct((depth, points // 2), jnp.bfloat16)],
        compiler_params=limit(LOAD_MIB),
        cost_estimate=pl.CostEstimate(flops=0, bytes_accessed=2 * orbitals.size, transcendentals=0),
        name="load",
    )(orbitals, sent)


def quarter_weights(own, chunks, depth, n_k, d_rows, c_part, far, *more):
    outs = [jax.ShapeDtypeStruct((n_k, c_part.shape[1] // 2), jnp.float32)] * 2
    return pl.pallas_call(
        functools.partial(weights_kernel, own, chunks, TILE, depth),
        in_specs=[VMEM] * 3 + [ANY] * len(more),
        out_specs=[VMEM] * len(outs),
        scratch_shapes=[],
        out_shape=outs,
        compiler_params=limit(WEIGHTS_MIB),
        cost_estimate=pl.CostEstimate(
            flops=2 * d_rows.size * c_part.shape[1], bytes_accessed=0, transcendentals=0
        ),
        name="weights",
    )(d_rows, c_part, far, *more)


def split(x):
    high = x.astype(jnp.bfloat16)
    rest = x - high.astype(jnp.float32)
    middle = rest.astype(jnp.bfloat16)
    low = (rest - middle.astype(jnp.float32)).astype(jnp.bfloat16)
    return high, middle, low


def outer_kernel(scale, *refs):
    *rows, columns, out_hbm, buffer, sems = refs
    core, parity = lax.axis_index("rep"), lax.axis_index("aux") % 2
    high, middle, low = split(columns[...] * scale)
    right = jnp.concatenate([high, middle, high, low, middle, high], axis=0)
    copies = []
    for i, weights in enumerate(rows):
        block = weights.shape[1]
        half = 1 - parity if i % 2 else parity
        side = 1 - core if i // 2 else core
        step = min(block, ROWS)
        for lo in range(0, block, step):
            high, middle, low = split(weights[:, lo : lo + step])
            left = jnp.concatenate([high, high, middle, high, middle, low], axis=0)
            here = pl.ds(i * block + lo, step)
            buffer[here, :] = lax.dot_general(
                left, right, (((0,), (0,)), ((), ())), preferred_element_type=jnp.float32
            )
            to = pl.ds(pl.multiple_of((half * 2 + side) * block + lo, 8), step)
            copy = pltpu.make_async_copy(buffer.at[here], out_hbm.at[to], sems.at[len(copies)])
            copy.start()
            copies.append(copy)
    for copy in copies:
        copy.wait()


def outer(rows, columns, out_shape):
    n_k, width = columns.shape
    return pl.pallas_call(
        functools.partial(outer_kernel, 1.0 / n_k),
        in_specs=[VMEM] * (len(rows) + 1),
        out_specs=ANY,
        scratch_shapes=[pltpu.VMEM(out_shape, jnp.float32), pltpu.SemaphoreType.DMA((32,))],
        out_shape=jax.ShapeDtypeStruct(out_shape, jnp.float32),
        compiler_params=limit(OUTER_MIB),
        cost_estimate=pl.CostEstimate(
            flops=2 * 6 * n_k * out_shape[0] * width, bytes_accessed=4 * out_shape[0] * width, transcendentals=0
        ),
        name="outer",
    )(*rows, columns)


def swap(x):
    return lax.ppermute(x, "rep", [(0, 1), (1, 0)])


def from_aux(x, n_aux, shift):
    return lax.ppermute(x, "aux", [(i, i ^ shift) for i in range(n_aux)])


def per_device(n_aux, n_pts, density_slab, orbitals):
    aux, pts = lax.axis_index("aux"), lax.axis_index("pts")
    n_k, depth, q = density_slab.shape
    points = orbitals.shape[1]
    block = points // 4
    chunks = [(0, block)]
    d_rows = density_slab.reshape(-1, ROWS, q)

    sent = first_rows(orbitals, depth)
    far_first = swap(sent)
    c_first, c_second, sent = load(orbitals, sent, depth)
    far_second = swap(sent)
    sends = quarter_weights(False, chunks, depth, n_k, d_rows, c_first, far_first)
    came = [swap(x) for x in sends]
    keeps = quarter_weights(True, chunks, depth, n_k, d_rows, c_second, far_second)
    mine, cross = lax.optimization_barrier([x + y for x, y in zip(keeps, came)])

    a_total = mine
    for shift in [n_aux // 2] + [i for i in range(1, n_aux) if i != n_aux // 2]:
        a_total = a_total + from_aux(cross if shift % 2 else mine, n_aux, shift)
    b_total = cross + from_aux(mine, n_aux, 1)
    shift = 2
    while shift < n_aux:
        b_total = b_total + from_aux(b_total, n_aux, shift)
        shift *= 2

    home = n_aux // n_pts

    def columns_of(held):
        got = held
        for shift in range(1, n_pts):
            came = lax.ppermute(held, "pts", [(i, (i + shift) % n_pts) for i in range(n_pts)])
            got = jnp.where((pts - aux // home) % n_pts == shift, came, got)
        return got

    columns = columns_of(a_total)
    rows = [a_total, b_total, swap(a_total), swap(b_total)]
    return outer(rows, columns, (points, block))


def solution(mesh):
    shape = mesh.shape
    return jax.shard_map(
        functools.partial(per_device, shape["aux"], shape["pts"]),
        mesh=mesh,
        in_specs=(P("groups", "aux", "rep"), P(("groups", "rep"), "pts")),
        out_specs=P(("groups", "pts"), ("aux", "rep")),
        check_vma=False,
    )
```

```python
import functools

import jax
import jax.numpy as jnp
from jax import lax
from jax.experimental import pallas as pl
from jax.experimental.pallas import tpu as pltpu
from jax.sharding import PartitionSpec as P

MIB = 1 << 20
ROWS = 256
SLICE_MIB = 50
LOAD_MIB = 44
WEIGHTS_MIB = 36
OUTER_MIB = 40
TILE = 512


def first_kernel(c_hbm, rows_ref, sems):
    depth, points = rows_ref.shape
    place = Place(depth, points)
    copies = place.copies(1, c_hbm.at[place.rows], rows_ref, sems)
    for copy in copies:
        copy.start()
    for copy in copies:
        copy.wait()


def load_kernel(c_hbm, sent, c_ref, next_ref, rows_ref, sems):
    depth, points = rows_ref.shape
    place = Place(depth, points)
    first = place.copies(0, c_hbm, c_ref, sems.at[pl.ds(0, 2)])
    second = place.copies(1, c_hbm, next_ref, sems.at[pl.ds(2, 2)])
    rows = pltpu.make_async_copy(c_ref.at[place.rows], rows_ref, sems.at[4])
    for copy in first + second:
        copy.start()
    for copy in first:
        copy.wait()
    rows.start()
    for copy in second:
        copy.wait()
    rows.wait()


class Place:
    def __init__(self, depth, points):
        self.core = lax.axis_index("rep")
        aux = lax.axis_index("aux")
        per_core = lax.axis_size("aux") // 2
        self.near = aux // per_core == self.core
        self.rows = pl.ds(pl.multiple_of(aux % per_core * depth, 16), depth)
        self.parity = aux % 2
        self.block = points // 2

    def copies(self, own, source, target, sems):
        core = self.core if own else 1 - self.core
        return [
            pltpu.make_async_copy(
                source.at[:, pl.ds(pl.multiple_of(((i + self.parity) % 2 * 2 + core) * self.block, 128), self.block)],
                target.at[:, pl.ds(i * self.block, self.block)],
                sems.at[i],
            )
            for i in range(2)
        ]


def weights_kernel(own, chunks, tile, depth, d_ref, c_ref, far_ref, *refs):
    n_groups, rows, _ = d_ref.shape
    span = rows // depth
    points = c_ref.shape[1]
    block = points // 2
    place = Place(depth, points)
    for half, w_ref in enumerate(refs):
        for start, width in chunks:
            for lo in range(0, width, tile):
                size = min(tile, width - lo)
                there = slice(half * block + start + lo, half * block + start + lo + size)
                scale = jnp.where(place.near, c_ref[place.rows, there], far_ref[:, there]).astype(jnp.float32)
                for g in range(n_groups):
                    product = jnp.dot(d_ref[g], c_ref[:, there], preferred_element_type=jnp.float32)
                    w_ref[g * span : (g + 1) * span, lo : lo + size] = jnp.sum(
                        product.reshape(span, depth, size) * scale[None], axis=1
                    )


VMEM = pl.BlockSpec(memory_space=pltpu.VMEM)
ANY = pl.BlockSpec(memory_space=pl.ANY)


def limit(mib):
    return pltpu.CompilerParams(vmem_limit_bytes=mib * MIB)


def first_rows(orbitals, depth):
    return pl.pallas_call(
        first_kernel,
        in_specs=[ANY],
        out_specs=VMEM,
        scratch_shapes=[pltpu.SemaphoreType.DMA((2,))],
        out_shape=jax.ShapeDtypeStruct((depth, orbitals.shape[1] // 2), jnp.bfloat16),
        compiler_params=limit(SLICE_MIB),
        name="first_rows",
    )(orbitals)


def load(orbitals, sent, depth):
    q, points = orbitals.shape
    part = jax.ShapeDtypeStruct((q, points // 2), jnp.bfloat16)
    return pl.pallas_call(
        load_kernel,
        in_specs=[ANY, ANY],
        out_specs=[VMEM] * 3,
        scratch_shapes=[pltpu.SemaphoreType.DMA((5,))],
        out_shape=[part, part, jax.ShapeDtypeStruct((depth, points // 2), jnp.bfloat16)],
        compiler_params=limit(LOAD_MIB),
        cost_estimate=pl.CostEstimate(flops=0, bytes_accessed=2 * orbitals.size, transcendentals=0),
        name="load",
    )(orbitals, sent)


def quarter_weights(own, chunks, depth, n_k, d_rows, c_part, far, *more):
    outs = [jax.ShapeDtypeStruct((n_k, c_part.shape[1] // 2), jnp.float32)] * 2
    return pl.pallas_call(
        functools.partial(weights_kernel, own, chunks, TILE, depth),
        in_specs=[VMEM] * 3 + [ANY] * len(more),
        out_specs=[VMEM] * len(outs),
        scratch_shapes=[],
        out_shape=outs,
        compiler_params=limit(WEIGHTS_MIB),
        cost_estimate=pl.CostEstimate(
            flops=2 * d_rows.size * c_part.shape[1], bytes_accessed=0, transcendentals=0
        ),
        name="weights",
    )(d_rows, c_part, far, *more)


def split(x):
    high = x.astype(jnp.bfloat16)
    rest = x - high.astype(jnp.float32)
    middle = rest.astype(jnp.bfloat16)
    low = (rest - middle.astype(jnp.float32)).astype(jnp.bfloat16)
    return high, middle, low


def outer_kernel(scale, *refs):
    *rows, columns, out_hbm, buffer, sems = refs
    core, parity = lax.axis_index("rep"), lax.axis_index("aux") % 2
    high, middle, low = split(columns[...] * scale)
    right = jnp.concatenate([high, middle, high, low, middle, high], axis=0)
    copies = []
    for i, weights in enumerate(rows):
        block = weights.shape[1]
        half = 1 - parity if i % 2 else parity
        side = 1 - core if i // 2 else core
        cuts = sorted({0, *([128] if i == 0 and block > 128 else []), *range(0, block, ROWS), block})
        for lo, hi in zip(cuts, cuts[1:]):
            step = hi - lo
            high, middle, low = split(weights[:, lo : lo + step])
            left = jnp.concatenate([high, high, middle, high, middle, low], axis=0)
            here = pl.ds(i * block + lo, step)
            buffer[here, :] = lax.dot_general(
                left, right, (((0,), (0,)), ((), ())), preferred_element_type=jnp.float32
            )
            to = pl.ds(pl.multiple_of((half * 2 + side) * block + lo, 8), step)
            copy = pltpu.make_async_copy(buffer.at[here], out_hbm.at[to], sems.at[len(copies)])
            copy.start()
            copies.append(copy)
    for copy in copies:
        copy.wait()


def outer(rows, columns, out_shape):
    n_k, width = columns.shape
    return pl.pallas_call(
        functools.partial(outer_kernel, 1.0 / n_k),
        in_specs=[VMEM] * (len(rows) + 1),
        out_specs=ANY,
        scratch_shapes=[pltpu.VMEM(out_shape, jnp.float32), pltpu.SemaphoreType.DMA((32,))],
        out_shape=jax.ShapeDtypeStruct(out_shape, jnp.float32),
        compiler_params=limit(OUTER_MIB),
        cost_estimate=pl.CostEstimate(
            flops=2 * 6 * n_k * out_shape[0] * width, bytes_accessed=4 * out_shape[0] * width, transcendentals=0
        ),
        name="outer",
    )(*rows, columns)


def swap(x):
    return lax.ppermute(x, "rep", [(0, 1), (1, 0)])


def from_aux(x, n_aux, shift):
    return lax.ppermute(x, "aux", [(i, i ^ shift) for i in range(n_aux)])


def per_device(n_aux, n_pts, density_slab, orbitals):
    aux, pts = lax.axis_index("aux"), lax.axis_index("pts")
    n_k, depth, q = density_slab.shape
    points = orbitals.shape[1]
    block = points // 4
    chunks = [(0, block)]
    d_rows = density_slab.reshape(-1, ROWS, q)

    sent = first_rows(orbitals, depth)
    far_first = swap(sent)
    c_first, c_second, sent = load(orbitals, sent, depth)
    far_second = swap(sent)
    sends = quarter_weights(False, chunks, depth, n_k, d_rows, c_first, far_first)
    came = [swap(x) for x in sends]
    keeps = quarter_weights(True, chunks, depth, n_k, d_rows, c_second, far_second)
    mine, cross = lax.optimization_barrier([x + y for x, y in zip(keeps, came)])

    a_total = mine
    for shift in [n_aux // 2] + [i for i in range(1, n_aux) if i != n_aux // 2]:
        a_total = a_total + from_aux(cross if shift % 2 else mine, n_aux, shift)
    b_total = cross + from_aux(mine, n_aux, 1)
    shift = 2
    while shift < n_aux:
        b_total = b_total + from_aux(b_total, n_aux, shift)
        shift *= 2

    home = n_aux // n_pts

    def columns_of(held):
        got = held
        for shift in range(1, n_pts):
            came = lax.ppermute(held, "pts", [(i, (i + shift) % n_pts) for i in range(n_pts)])
            got = jnp.where((pts - aux // home) % n_pts == shift, came, got)
        return got

    columns = columns_of(a_total)
    rows = [a_total, b_total, swap(a_total), swap(b_total)]
    return outer(rows, columns, (points, block))


def solution(mesh):
    shape = mesh.shape
    return jax.shard_map(
        functools.partial(per_device, shape["aux"], shape["pts"]),
        mesh=mesh,
        in_specs=(P("groups", "aux", "rep"), P(("groups", "rep"), "pts")),
        out_specs=P(("groups", "pts"), ("aux", "rep")),
        check_vma=False,
    )
```
